512 devices in a mesh: pp: 16 (over z), ep: 32 (over y, x, core).
Axes of the slice: x: 4, y: 4, z: 16, core: 2. Of those that a mesh axis runs over, the one named last changes fastest.
Arguments:
- fwd_act: bfloat16 [32768, 3584], P(('pp', 'ep')), may hold values from -6 to 6
- fwd_ids: int32 [32768, 1], P(('pp', 'ep')), may hold values from 0 to 3; in each aligned block of 64 rows (0 to 63, 64 to 127, ...) at most 17 rows name the same one
- bwd_act: bfloat16 [32768, 3584], P(('pp', 'ep')), may hold values from -6 to 6
- bwd_ids: int32 [32768, 1], P(('pp', 'ep')), may hold values from 0 to 3; in each aligned block of 64 rows (0 to 63, 64 to 127, ...) at most 17 rows name the same one
- bwd_grad: bfloat16 [32768, 3584], P(('pp', 'ep')), may hold values from -6 to 6
- norm_gain: bfloat16 [16, 3584], P('pp'), may hold values from 0.099609375 to 1.8984375
- router: bfloat16 [16, 3584, 4], P('pp'), may hold values from -0.09375 to 0.09375
- w_gate: bfloat16 [512, 3584, 128], P(('pp', 'ep')), may hold values from -0.09375 to 0.09375
- w_down: bfloat16 [512, 128, 3584], P(('pp', 'ep')), may hold values from -0.1875 to 0.1875
- saved_gate: bfloat16 [16, 32, 544, 128], P('pp', 'ep'), may hold values from -6 to 6
Outputs:
- fwd_next: bfloat16 [32768, 3584], P(('pp', 'ep'))
- bwd_next: bfloat16 [32768, 3584], P(('pp', 'ep'))
The draws below stay inside these ranges and needn't reach their ends.
Inputs may be any that keep to these rules, and one draw needn't show every extreme that they name: `fwd_ids`: each row names one held expert. Among the rows of one device no expert is named by more than 17 rows; some device names some expert exactly 17 times. `bwd_ids`: as for fwd_ids.
All inputs are finite; a program needn't handle non-finite values.
Results may differ from the reference program's by a relative error of at most 0.015.
Values may be sent and summed in bfloat16 or wider, within the bound.
A program may use at most 128 MiB of HBM per device.

```python
import math
import jax
import jax.numpy as jnp
import numpy as np
from jax import lax

D = 3584
HID = 1024
EXPERTS = 4
TOPK = 1
TOK_DEV = 64
HSPLIT = 8
HSLICE = 128
CAP = 17
TOKENS = 2048
N_PP = 16
N_EP = 32


def shard_levels(rng, extent, cuts, least, high):
    gain = 1.0
    for position, shards_of in cuts:
        steps = jax.random.uniform(jax.random.fold_in(jax.random.fold_in(rng, 6), position), (shards_of,), jnp.float32, least / len(cuts), high / len(cuts))
        gain = gain * jnp.repeat(jnp.exp(steps), extent[position] // shards_of).reshape((-1,) + (1,) * (len(extent) - 1 - position))
    return gain


def routed_block(stream_key, own, number, rows, number_of, top, most, skew):
    ranking = jax.random.permutation(stream_key, number_of)
    packed, usual = shares(number_of, rows * top, most, skew, True), shares(number_of, rows * top, most, skew, False)
    places = jnp.arange(number_of)

    def named(tallies, rotation):
        used = int((tallies > 0).sum())
        fixed = max(1, used // 4)
        passed = fixed + (places - fixed + rotation * (used - fixed)) % max(1, number_of - fixed)
        return jnp.zeros((number_of,), jnp.int32).at[ranking[jnp.where(places < fixed, places, passed)]].set(jnp.asarray(tallies, jnp.int32))

    tallies = jnp.where(number % 4 == 0, named(packed, number // 4), named(usual, number - number // 4 - 1))
    mixed = jax.random.permutation(jax.random.fold_in(own, 3), number_of)
    donor, taker = mixed[0:number_of // 2 * 2:2], mixed[1:number_of // 2 * 2:2]
    margin = jnp.minimum(tallies[donor] - 1, most - tallies[taker]) // 2
    margin = jnp.where((donor == ranking[0]) | (taker == ranking[0]) | (tallies[taker] == 0), 0, jnp.maximum(margin, 0))
    passed = jax.random.randint(jax.random.fold_in(own, 4), (number_of // 2,), 0, 1 << 20) % (margin + 1)
    tallies = tallies.at[donor].add(-passed).at[taker].add(passed)
    items = jnp.searchsorted(jnp.cumsum(tallies), jnp.arange(rows * top), side="right").astype(jnp.int32)
    listing = items.reshape(top, rows).T
    listing = listing[jax.random.permutation(jax.random.fold_in(own, 1), rows)]
    rotation = jax.random.randint(jax.random.fold_in(own, 2), (rows, 1), 0, top)
    return jnp.take_along_axis(listing, (jnp.arange(top)[None, :] + rotation) % top, axis=1)


def shares(number_of, total, limit, skew, full):
    loads = [(1 << 20) // math.isqrt(standing ** skew) + 1 for standing in range(1, number_of + 1)]
    largest = limit if full else min(limit, max(-(-total // number_of), total * loads[0] // sum(loads)))
    least = 1 if total - largest >= number_of - 1 else 0
    counts, spare = [largest] + [least] * (number_of - 1), total - largest - least * (number_of - 1)
    while spare > 0:
        movable = [i for i in range(1, number_of) if counts[i] < largest] or [i for i in range(1, number_of) if counts[i] < limit]
        whole, left = sum([loads[i] for i in movable]), spare
        for i in movable:
            more = min(limit - counts[i], max(1, left * loads[i] // whole), spare)
            counts[i] = counts[i] + more
            spare = spare - more
    return np.array(counts)


def centred(stream_key, shape, deviation, reach, cuts=(), kind=jnp.bfloat16):
    drawn = deviation * jax.random.normal(stream_key, shape, jnp.float32)
    if cuts:
        drawn = drawn * shard_levels(stream_key, shape, cuts, -0.22, 0.18)
    return jnp.clip(drawn, -reach, reach).astype(kind)


def setup_inputs(seed: int = 0) -> dict:
    splits = jax.random.split(jax.random.key(seed), 11)
    fwd_act = centred(splits[0], (N_PP * TOKENS, D), 1.0, 6.0, ((0, 512),))
    fwd_ids_keys = jax.random.split(jax.random.fold_in(splits[1], 1), (N_PP * TOKENS) // TOK_DEV)
    fwd_ids_turns = jax.random.permutation(jax.random.fold_in(splits[1], 3), (N_PP * TOKENS) // TOK_DEV)
    fwd_ids = jax.vmap(lambda own, number: routed_block(jax.random.fold_in(splits[1], 2), own, number, TOK_DEV, EXPERTS, TOPK, CAP, 2))(fwd_ids_keys, fwd_ids_turns).reshape((N_PP * TOKENS, TOPK))
    bwd_act = centred(splits[2], (N_PP * TOKENS, D), 1.0, 6.0, ((0, 512),))
    bwd_ids_keys = jax.random.split(jax.random.fold_in(splits[3], 1), (N_PP * TOKENS) // TOK_DEV)
    bwd_ids_turns = jax.random.permutation(jax.random.fold_in(splits[3], 3), (N_PP * TOKENS) // TOK_DEV)
    bwd_ids = jax.vmap(lambda own, number: routed_block(jax.random.fold_in(splits[3], 2), own, number, TOK_DEV, EXPERTS, TOPK, CAP, 2))(bwd_ids_keys, bwd_ids_turns).reshape((N_PP * TOKENS, TOPK))
    bwd_grad = centred(splits[4], (N_PP * TOKENS, D), 1.0, 6.0, ((0, 512),))
    norm_gain = jnp.clip(1.0 + 0.18 * jax.random.normal(splits[5], (N_PP, D), jnp.float32), 0.099609375, 1.8984375).astype(jnp.bfloat16)
    router = centred(splits[6], (N_PP, D, EXPERTS), D ** -0.5, 0.09375, ((0, 16),))
    w_gate = centred(splits[7], (N_PP * N_EP, D, HSLICE), D ** -0.5, 0.09375, ((0, 512),))
    w_down = centred(splits[8], (N_PP * N_EP, HSLICE, D), HID ** -0.5, 0.1875, ((0, 512),))
    saved_gate = centred(splits[9], (N_PP, N_EP, N_EP * CAP, HSLICE), 1.0, 6.0, ((0, 16), (1, 32)))
    return {"fwd_act": fwd_act, "fwd_ids": fwd_ids, "bwd_act": bwd_act, "bwd_ids": bwd_ids, "bwd_grad": bwd_grad, "norm_gain": norm_gain, "router": router, "w_gate": w_gate, "w_down": w_down, "saved_gate": saved_gate}


epsilon = 1e-06
route_scale = 2.5

def normalize(act, gain_row):
    values = act.astype(jnp.float32)
    scaled = lax.rsqrt(lax.optimization_barrier(jnp.mean(values * values, axis=-1, keepdims=True)) + epsilon)
    return ((values * scaled * gain_row.astype(jnp.float32)).astype(jnp.bfloat16), scaled)

def gating(normed, router_table, ids):
    logits = jnp.dot(normed, router_table, preferred_element_type=jnp.float32)
    affinity = jax.nn.sigmoid(logits)
    selected = (ids[:, :, None] == jnp.arange(router_table.shape[1], dtype=jnp.int32)[None, None, :]).astype(jnp.float32)
    gates = lax.optimization_barrier(jnp.sum(selected * affinity[:, None, :], axis=-1))
    return (gates, affinity, selected)

def positions(flat_ids, experts):
    onehot = (flat_ids[..., None] == jnp.arange(experts, dtype=jnp.int32)).astype(jnp.int32)
    earlier = jnp.cumsum(onehot, axis=-2) - onehot
    return lax.optimization_barrier(jnp.sum(earlier * onehot, axis=-1))

def slot_table(ids):
    flat_ids = ids.reshape(N_EP, TOK_DEV * TOPK)
    place = positions(flat_ids, EXPERTS)
    source = jnp.arange(N_EP, dtype=jnp.int32)[:, None]
    token = source * TOK_DEV + jnp.arange(TOK_DEV * TOPK, dtype=jnp.int32)[None, :] // TOPK
    slot_index = flat_ids * (N_EP * CAP) + source * CAP + place
    owner = jnp.full((EXPERTS * N_EP * CAP,), TOKENS, jnp.int32).at[slot_index.reshape(-1)].set(token.reshape(-1))
    return (owner, slot_index.reshape(TOKENS, TOPK))

def collect(rows, owner):
    padded = jnp.concatenate([rows, jnp.zeros((1, D), rows.dtype)], axis=0)
    return padded[owner].reshape(EXPERTS, N_EP * CAP, D)

def experts_forward(slot_rows, gate_parts, down_parts):
    rows_wide = slot_rows.astype(jnp.float32)

    def add_slice(total, parts):
        gate_proj = jnp.einsum('erd,edh->erh', rows_wide, parts[0].astype(jnp.float32))
        hidden = jax.nn.silu(gate_proj).astype(jnp.bfloat16)
        output = jnp.einsum('erh,ehd->erd', hidden.astype(jnp.float32), parts[1].astype(jnp.float32)).astype(jnp.bfloat16)
        return (total + output.astype(jnp.float32), None)
    total, unused = lax.scan(add_slice, jnp.zeros(slot_rows.shape, jnp.float32), (gate_parts, down_parts))
    return total

def experts_backward(slot_grads, saved_parts, gate_parts, down_parts):
    grads_wide = slot_grads.astype(jnp.float32)

    def add_slice(totals, parts):
        gate_proj = parts[0].astype(jnp.float32)
        down_wide = parts[2].astype(jnp.float32)
        hidden = jax.nn.silu(gate_proj).astype(jnp.bfloat16)
        output = jnp.einsum('erh,ehd->erd', hidden.astype(jnp.float32), down_wide).astype(jnp.bfloat16)
        dot_part = lax.optimization_barrier(jnp.sum(grads_wide * output.astype(jnp.float32), axis=-1)).astype(jnp.bfloat16)
        grad_hidden = jnp.einsum('erd,ehd->erh', grads_wide, down_wide)
        sigmoid_gate = jax.nn.sigmoid(gate_proj)
        grad_gate = (grad_hidden * sigmoid_gate * (1.0 + gate_proj * (1.0 - sigmoid_gate))).astype(jnp.bfloat16)
        grad_part = jnp.einsum('erh,edh->erd', grad_gate.astype(jnp.float32), parts[1].astype(jnp.float32)).astype(jnp.bfloat16)
        return ((totals[0] + grad_part.astype(jnp.float32), totals[1] + dot_part.astype(jnp.float32)), None)
    start = (jnp.zeros(slot_grads.shape, jnp.float32), jnp.zeros(slot_grads.shape[:2], jnp.float32))
    totals, unused = lax.scan(add_slice, start, (saved_parts, gate_parts, down_parts))
    return totals

def finish_forward(act, gates, gathered):
    mixed = lax.optimization_barrier(jnp.sum(gates[:, :, None] * gathered, axis=1))
    return (act.astype(jnp.float32) + route_scale * mixed).astype(jnp.bfloat16)

def finish_backward(act, grad, scaled, gain_row, router_table, gates, affinity, selected, grad_rows, dot_terms):
    route_coef = route_scale * gates
    grad_normed = lax.optimization_barrier(jnp.sum(route_coef[:, :, None] * grad_rows, axis=1))
    grad_gates = route_scale * dot_terms
    grad_affinity = lax.optimization_barrier(jnp.sum(selected * grad_gates[:, :, None], axis=1))
    grad_logits = (grad_affinity * affinity * (1.0 - affinity)).astype(jnp.bfloat16)
    grad_normed = grad_normed + jnp.dot(grad_logits, router_table.T, preferred_element_type=jnp.float32)
    values = act.astype(jnp.float32)
    grad_pre = grad_normed * gain_row.astype(jnp.float32)
    grad_act = scaled * (grad_pre - values * scaled * scaled * lax.optimization_barrier(jnp.mean(grad_pre * values, axis=-1, keepdims=True)))
    return (grad.astype(jnp.float32) + grad_act).astype(jnp.bfloat16)

def section_step(pieces):
    fwd_act, fwd_ids, bwd_act, bwd_ids, bwd_grad, gain_row, router_table, gate_section, down_section, saved_section = pieces
    gate_parts = gate_section.reshape(EXPERTS, HSPLIT, D, HSLICE).transpose(1, 0, 2, 3)
    down_parts = down_section.reshape(EXPERTS, HSPLIT, HSLICE, D).transpose(1, 0, 2, 3)
    saved_parts = saved_section.reshape(EXPERTS, HSPLIT, N_EP * CAP, HSLICE).transpose(1, 0, 2, 3)
    fwd_normed, fwd_scaled = normalize(fwd_act, gain_row)
    fwd_gates, fwd_aff, fwd_sel = gating(fwd_normed, router_table, fwd_ids)
    fwd_owner, fwd_slot = slot_table(fwd_ids)
    fwd_y = experts_forward(collect(fwd_normed, fwd_owner), gate_parts, down_parts)
    fwd_gathered = fwd_y.reshape(-1, D)[fwd_slot]
    fwd_result = finish_forward(fwd_act, fwd_gates, fwd_gathered)
    bwd_normed, bwd_scaled = normalize(bwd_act, gain_row)
    bwd_gates, bwd_aff, bwd_sel = gating(bwd_normed, router_table, bwd_ids)
    bwd_owner, bwd_slot = slot_table(bwd_ids)
    grad_rows, dot_terms = experts_backward(collect(bwd_grad, bwd_owner), saved_parts, gate_parts, down_parts)
    bwd_rows = grad_rows.reshape(-1, D)[bwd_slot]
    bwd_dots = dot_terms.reshape(-1)[bwd_slot]
    bwd_result = finish_backward(bwd_act, bwd_grad, bwd_scaled, gain_row, router_table, bwd_gates, bwd_aff, bwd_sel, bwd_rows, bwd_dots)
    return (fwd_result, bwd_result)

def reference(fwd_act, fwd_ids, bwd_act, bwd_ids, bwd_grad, norm_gain, router, w_gate, w_down, saved_gate):

    def split(arr):
        return arr.reshape((N_PP, arr.shape[0] // N_PP) + arr.shape[1:])
    pieces = (split(fwd_act), split(fwd_ids), split(bwd_act), split(bwd_ids), split(bwd_grad), norm_gain, router, split(w_gate), split(w_down), saved_gate)
    fwd_result, bwd_result = lax.map(section_step, pieces)
    fwd_next = jnp.roll(fwd_result, 1, axis=0).reshape(N_PP * TOKENS, D)
    bwd_next = jnp.roll(bwd_result, -1, axis=0).reshape(N_PP * TOKENS, D)
    return (fwd_next, bwd_next)
```

```python
import functools

import jax
import jax.numpy as jnp
from jax import lax
from jax.experimental import pallas as pl
from jax.experimental.pallas import tpu as pltpu
from jax.sharding import PartitionSpec as P

MESH = pl.DeviceIdType.MESH
bf16 = jnp.bfloat16
f32 = jnp.float32
epsilon = 1e-06
route_scale = 2.5

TOK = 64
CAP = 17
EXP = 4
PACK = 48
BLK = 144
DOTROW = 34
HS = 128
NCH = 2
MIRROR = (0, 2, 1, 3)


def iota(shape, dim):
    return lax.broadcasted_iota(jnp.int32, shape, dim)


def mm(a, b):
    return lax.dot_general(a, b, (((1,), (0,)), ((), ())), preferred_element_type=f32)


def mm_nt(a, b):
    return lax.dot_general(a, b, (((1,), (1,)), ((), ())), preferred_element_type=f32)


def group_of(q):
    return (q >= 17).astype(jnp.int32) + (q >= 34).astype(jnp.int32) + (q >= 51).astype(jnp.int32)


def kernel(
    fa, fid, ba, bid, bg, gain, rt, wg_hbm, wd_hbm, saved,
    fout, bout,
    S, RY, A, WG, WD, zo, zs, zr, hs, hr, o3, relay, o1, o2, fup, fdn, TS, TR,
    fst, bst, gpre, svp, oh, dots,
    wl, wsend, wrecv, dloc, dsend, drecv, asend, arecv, zsend, zrecv, hsend, hrecv,
    rsend, rrecv, tloc, tsend, trecv, osend, orecv,
):
    D = fa.shape[1]
    HF = D // 2
    CW = HF // NCH
    n_pp = lax.axis_size("pp")
    pp = lax.axis_index("pp")
    ep = lax.axis_index("ep")
    y = ep // 8
    x = (ep // 2) % 4
    c = ep % 2

    def dev(yy, xx, cc):
        return (pp, (yy * 4 + xx) * 2 + cc)

    up = 1 + 2 * c
    x_up = (x + up) % 4
    x_dn = (x + 4 - up) % 4
    x_op = (x + 2) % 4
    d_up = dev(y, x_up, c)
    d_dn = dev(y, x_dn, c)
    d_sib = dev(y, x, 1 - c)
    d_zn = ((pp + 1) % n_pp, ep)
    d_zp = ((pp + n_pp - 1) % n_pp, ep)
    others = [(dy, dc) for dy in range(4) for dc in range(2) if (dy, dc) != (0, 0)]

    def remote(src, dst, ssem, rsem, device):
        return pltpu.make_async_remote_copy(
            src_ref=src, dst_ref=dst, send_sem=ssem, recv_sem=rsem, device_id=device, device_id_type=MESH
        )

    barrier = pltpu.get_barrier_semaphore()
    partners = [dev((y + dy) % 4, x, (c + dc) % 2) for dy, dc in others] + [d_up, d_dn, d_zn, d_zp]
    for partner in partners:
        pl.semaphore_signal(barrier, inc=1, device_id=partner, device_id_type=MESH)

    mine = pl.multiple_of(c * HF, 128)
    yours = pl.multiple_of((1 - c) * HF, 128)
    own_w = [
        pltpu.make_async_copy(wg_hbm.at[pl.ds(mine, HF), :], WG.at[:, pl.ds(0, HS)], wl.at[0]),
        pltpu.make_async_copy(wd_hbm.at[:, pl.ds(mine, HF)], WD.at[pl.ds(0, HS), :], wl.at[1]),
    ]
    for copy in own_w:
        copy.start()

    def cols(k):
        return slice(k * CW, (k + 1) * CW)

    def inverse(h_ref):
        total = jnp.zeros((TOK, 1), f32)
        for k in range(2 * NCH):
            v = h_ref[:, cols(k)].astype(f32)
            total = total + jnp.sum(v * v, axis=-1, keepdims=True)
        return lax.rsqrt(total * (1.0 / D) + epsilon)

    def normed(h_ref, inv, k):
        return (h_ref[:, cols(k)].astype(f32) * inv * gain[:, cols(k)].astype(f32)).astype(bf16)

    below = (iota((TOK, TOK), 0) > iota((TOK, TOK), 1)).astype(f32).astype(bf16)

    def routes(id_ref, base):
        ids = id_ref[...]
        onehot = (ids == iota((TOK, 16), 1)).astype(f32)
        earlier = mm(below, onehot.astype(bf16))
        place = jnp.sum(onehot * earlier, axis=-1, keepdims=True)
        column = ids.astype(f32) * PACK + place + base
        spread = (column == iota((TOK, 256), 1).astype(f32)).astype(f32)
        return onehot, place, spread

    f_one, f_place, f_spread = routes(fid, 0.0)
    b_one, b_place, b_spread = routes(bid, 17.0)
    spread = jnp.concatenate([f_spread, b_spread], axis=0)
    oh[...] = spread.astype(bf16)
    packer = spread.T[: EXP * PACK].astype(bf16)
    f_inv = inverse(fa)

    def send_desc(ch, dy, dc):
        e, c2 = (y + dy) % 4, (c + dc) % 2
        return remote(S.at[ch, c2, e], RY.at[ch, c, y], dsend.at[ch, dy, dc], drecv.at[ch, c, y], dev(e, x, c2))

    def arrive(buf, sem):
        remote(buf, buf, sem, sem, d_sib).wait_recv()

    logits = jnp.zeros((TOK, 16), f32)
    for ch in range(NCH):
        for c2 in range(2):
            k = c2 * NCH + ch
            norm = normed(fa, f_inv, k)
            both = jnp.concatenate([norm, bg[:, cols(k)]], axis=0)
            S[ch, c2] = mm(packer, both).astype(bf16).reshape(EXP, PACK, CW)
            logits = logits + mm_nt(norm, rt[:, cols(k)])
        if ch == 0:
            pl.semaphore_wait(barrier, len(partners))
        for dy, dc in others:
            send_desc(ch, dy, dc).start()
        pltpu.make_async_copy(S.at[ch, c, y], RY.at[ch, c, y], dloc.at[ch]).start()
    give_w = [
        remote(wg_hbm.at[pl.ds(yours, HF), :], WG.at[:, pl.ds(HS, HS)], wsend.at[0], wrecv.at[0], d_sib),
        remote(wd_hbm.at[:, pl.ds(yours, HF)], WD.at[pl.ds(HS, HS), :], wsend.at[1], wrecv.at[1], d_sib),
    ]
    for copy in give_w:
        copy.start()
    f_gate = jnp.sum(f_one * jax.nn.sigmoid(logits), axis=-1, keepdims=True)

    r = iota((BLK, 1), 0)
    q = r - 68
    want = jnp.where(r < 68, r + 31 * group_of(r), jnp.where(r < 136, q + 31 * group_of(q) + 17, -1))
    compact = (want == iota((BLK, EXP * PACK), 1)).astype(f32).astype(bf16)

    def ag_own(ch):
        return [
            remote(A.at[0, ch], A.at[1, ch], asend.at[0, ch], arecv.at[0, ch], d_up),
            remote(A.at[0, ch], A.at[2, ch], asend.at[1, ch], arecv.at[1, ch], d_dn),
        ]

    def ag_on(ch):
        return remote(A.at[1, ch], A.at[3, ch], asend.at[2, ch], arecv.at[2, ch], d_up)

    for ch in range(NCH):
        for dy, dc in others:
            sy, sc = (y + dy) % 4, (c + dc) % 2
            arrive(RY.at[ch, sc, sy], drecv.at[ch, sc, sy])
        pltpu.make_async_copy(S.at[ch, c, y], RY.at[ch, c, y], dloc.at[ch]).wait()
        for sc in range(2):
            A[0, ch, sc * BLK : (sc + 1) * BLK] = mm(compact, RY[ch, sc].reshape(EXP * PACK, CW)).astype(bf16)
        for copy in ag_own(ch):
            copy.start()

    b_inv = inverse(ba)
    logits = jnp.zeros((TOK, 16), f32)
    for k in range(2 * NCH):
        logits = logits + mm_nt(normed(ba, b_inv, k), rt[:, cols(k)])
    b_aff = jax.nn.sigmoid(logits)
    b_gate = jnp.sum(b_one * b_aff, axis=-1, keepdims=True)
    svp[0 : saved.shape[0]] = saved[...]
    svp[saved.shape[0] :] = jnp.zeros((svp.shape[0] - saved.shape[0], HS), bf16)
    kind = iota((2 * BLK, 1), 0)
    kind = jnp.where(kind >= BLK, kind - BLK, kind)
    is_f = kind < 68
    saved_at = jnp.where((r >= 68) & (r < 136), q + 119 * group_of(q), -100000)

    for copy in own_w:
        copy.wait()
    arrive(WG.at[:, pl.ds(HS, HS)], wrecv.at[0])
    arrive(WD.at[pl.ds(HS, HS), :], wrecv.at[1])

    def z_copy(s):
        return remote(zs.at[s], zr.at[MIRROR[s]], zsend.at[s], zrecv.at[MIRROR[s]], d_sib)

    def h_copy(s):
        return remote(hs.at[s], hr.at[MIRROR[s]], hsend.at[s], hrecv.at[MIRROR[s]], d_sib)

    def project(s):
        zg = jnp.zeros((2 * BLK, 2 * HS), f32)
        zd = jnp.zeros((2 * BLK, 2 * HS), f32)
        for ch in range(NCH):
            rows = A[s, ch]
            zg = zg + mm(rows, WG[cols(ch), :])
            zd = zd + mm_nt(rows, WD[:, cols(ch)])
        z = jnp.where(is_f, zg, zd)
        zo[s] = z[:, :HS]
        zs[s] = z[:, HS:]
        z_copy(s).start()

    def activate(s, xs):
        arrive(zr.at[s], zrecv.at[s])
        z = zo[s] + zr[s]
        lanes = iota((BLK, svp.shape[0]), 1)
        picks = [
            (lanes - 17 * (xs * 2 + sc) == saved_at).astype(f32).astype(bf16) for sc in range(2)
        ]
        sv = mm(jnp.concatenate(picks, axis=0), svp[...])
        base = jnp.where(is_f, z, sv)
        sig = jax.nn.sigmoid(base)
        hid = (base * sig).astype(bf16)
        gg = (z * sig * (1.0 + sv * (1.0 - sig))).astype(bf16)
        hs[s] = jnp.where(is_f, hid.astype(f32), gg.astype(f32)).astype(bf16)
        h_copy(s).start()
        prod = jnp.where(is_f, 0.0, hid.astype(f32) * z)
        prod = jnp.concatenate([prod, jnp.zeros((96, HS), f32)], axis=0)
        dots[s] = lax.dot_general(
            jnp.ones((8, HS), f32), prod, (((1,), (1,)), ((), ())),
            preferred_element_type=f32, precision=lax.Precision.HIGHEST,
        )

    def produce(s, ch):
        h = jnp.concatenate([hs[s].astype(f32), hr[s].astype(f32)], axis=1)
        hf = jnp.where(is_f, h, 0.0).astype(bf16)
        hb = jnp.where(is_f, 0.0, h).astype(bf16)
        out = mm(hf, WD[:, cols(ch)]) + mm_nt(hb, WG[cols(ch), :])
        if ch == 0:
            spare = jnp.concatenate([dots[s], jnp.zeros((8, CW - 384), f32)], axis=1)
            out = jnp.concatenate([out[:136], spare, out[144:280], spare], axis=0)
        return out

    def down3(ch):
        return remote(o3.at[ch], relay.at[ch], rsend.at[0, ch], rrecv.at[0, ch], d_dn)

    def down1(ch):
        return remote(o1.at[ch], fup.at[ch], rsend.at[1, ch], rrecv.at[1, ch], d_dn)

    def up2(ch):
        return remote(o2.at[ch], fdn.at[ch], rsend.at[2, ch], rrecv.at[2, ch], d_up)

    project(0)
    for ch in range(NCH):
        arrive(A.at[1, ch], arecv.at[0, ch])
        ag_on(ch).start()
    activate(0, x)
    project(1)
    for ch in range(NCH):
        arrive(A.at[2, ch], arecv.at[1, ch])
    project(2)
    activate(1, x_dn)
    activate(2, x_up)
    arrive(hr.at[2], hrecv.at[2])
    for ch in range(NCH):
        o2[ch] = produce(2, ch).astype(bf16)
        up2(ch).start()
    for ch in range(NCH):
        arrive(A.at[3, ch], arecv.at[2, ch])
    project(3)
    activate(3, x_op)
    arrive(hr.at[3], hrecv.at[3])
    for ch in range(NCH):
        o3[ch] = produce(3, ch).astype(bf16)
        down3(ch).start()
    arrive(hr.at[1], hrecv.at[1])
    for ch in range(NCH):
        arrive(relay.at[ch], rrecv.at[0, ch])
        o1[ch] = (produce(1, ch) + relay[ch].astype(f32)).astype(bf16)
        down1(ch).start()
    arrive(hr.at[0], hrecv.at[0])

    k = iota((EXP * PACK, 1), 0)
    ky = (k >= 48).astype(jnp.int32) + (k >= 96).astype(jnp.int32) + (k >= 144).astype(jnp.int32)
    i = k - 48 * ky
    source = jnp.where(
        i < 17, 17 * ky + i, jnp.where(i < 34, 51 + 17 * ky + i, jnp.where(i == DOTROW, 136, -1))
    )
    expand = (source == iota((EXP * PACK, BLK), 1)).astype(f32).astype(bf16)

    def back_desc(ch, dy, dc):
        ty, tc = (y + dy) % 4, (c + dc) % 2
        return remote(TS.at[ch, tc, ty], TR.at[ch, c, y], tsend.at[ch, dy, dc], trecv.at[ch, c, y], dev(ty, x, tc))

    for ch in range(NCH):
        out = produce(0, ch)
        arrive(fdn.at[ch], rrecv.at[2, ch])
        arrive(fup.at[ch], rrecv.at[1, ch])
        out = (out + fdn[ch].astype(f32) + fup[ch].astype(f32)).astype(bf16)
        for sc in range(2):
            TS[ch, sc] = mm(expand, out[sc * BLK : (sc + 1) * BLK]).astype(bf16).reshape(EXP, PACK, CW)
        for dy, dc in others:
            back_desc(ch, dy, dc).start()
        pltpu.make_async_copy(TS.at[ch, c, y], TR.at[ch, c, y], tloc.at[ch]).start()

    def fwd_copy(kk):
        return remote(fst.at[:, cols(kk)], fout.at[:, cols(kk)], osend.at[0, kk], orecv.at[0, kk], d_zn)

    def bwd_copy(kk):
        return remote(bst.at[:, cols(kk)], bout.at[:, cols(kk)], osend.at[1, kk], orecv.at[1, kk], d_zp)

    spots = oh[:, : EXP * PACK]
    mean = jnp.zeros((TOK, 1), f32)
    for ch in range(NCH):
        for dy, dc in others:
            ey, hc = (y + dy) % 4, (c + dc) % 2
            arrive(TR.at[ch, hc, ey], trecv.at[ch, hc, ey])
        pltpu.make_async_copy(TS.at[ch, c, y], TR.at[ch, c, y], tloc.at[ch]).wait()
        if ch == 0:
            where_dot = (144 * c + 68 + 17 * y).astype(f32) + b_place
            hit = where_dot == iota((TOK, 384), 1).astype(f32)
            dot = jnp.zeros((TOK, 1), f32)
            for e in range(EXP):
                both = TR[0, 0, e, 32:48, 0:384].astype(f32) + TR[0, 1, e, 32:48, 0:384].astype(f32)
                found = jnp.sum(jnp.where(hit, both[2:3, :], 0.0), axis=-1, keepdims=True)
                dot = dot + b_one[:, e : e + 1] * found
            grad_aff = b_one * (route_scale * dot)
            grad_logits = (grad_aff * b_aff * (1.0 - b_aff)).astype(bf16)
        for c2 in range(2):
            kk = c2 * NCH + ch
            got = mm(spots, TR[ch, c2].reshape(EXP * PACK, CW))
            fst[:, cols(kk)] = (
                fa[:, cols(kk)].astype(f32) + route_scale * (f_gate * got[:TOK])
            ).astype(bf16)
            fwd_copy(kk).start()
            grad_n = (route_scale * b_gate) * got[TOK:] + mm(grad_logits, rt[:, cols(kk)])
            pre = grad_n * gain[:, cols(kk)].astype(f32)
            gpre[:, cols(kk)] = pre
            mean = mean + jnp.sum(pre * ba[:, cols(kk)].astype(f32), axis=-1, keepdims=True)
    factor = b_inv * b_inv * (mean * (1.0 / D))
    for kk in range(2 * NCH):
        grad = b_inv * (gpre[:, cols(kk)] - ba[:, cols(kk)].astype(f32) * factor)
        bst[:, cols(kk)] = (bg[:, cols(kk)].astype(f32) + grad).astype(bf16)
        bwd_copy(kk).start()

    for copy in give_w:
        copy.wait_send()
    for ch in range(NCH):
        for dy, dc in others:
            send_desc(ch, dy, dc).wait_send()
            back_desc(ch, dy, dc).wait_send()
        for copy in ag_own(ch):
            copy.wait_send()
        ag_on(ch).wait_send()
        down3(ch).wait_send()
        down1(ch).wait_send()
        up2(ch).wait_send()
    for s in range(4):
        z_copy(s).wait_send()
        h_copy(s).wait_send()
    for kk in range(2 * NCH):
        fwd_copy(kk).wait()
        bwd_copy(kk).wait()


def on_device(
    fwd_act, fwd_ids, bwd_act, bwd_ids, bwd_grad, norm_gain, router, w_gate, w_down, saved_gate
):
    D = fwd_act.shape[1]
    HF = D // 2
    CW = HF // NCH
    rt = jnp.pad(router[0].T, ((0, 12), (0, 0)))
    saved = saved_gate[0, 0]
    vmem = pl.BlockSpec(memory_space=pltpu.VMEM)
    hbm = pl.BlockSpec(memory_space=pl.ANY)
    dma = pltpu.SemaphoreType.DMA
    V = pltpu.VMEM
    block = (NCH, 2 * BLK, CW)
    return pl.pallas_call(
        kernel,
        out_shape=[jax.ShapeDtypeStruct((TOK, D), bf16)] * 2,
        in_specs=[vmem] * 7 + [hbm] * 2 + [vmem],
        out_specs=[hbm, hbm],
        scratch_shapes=[
            V((NCH, 2, EXP, PACK, CW), bf16),
            V((NCH, 2, EXP, PACK, CW), bf16),
            V((4,) + block, bf16),
            V((HF, 2 * HS), bf16),
            V((2 * HS, HF), bf16),
            V((4, 2 * BLK, HS), f32),
            V((4, 2 * BLK, HS), f32),
            V((4, 2 * BLK, HS), f32),
            V((4, 2 * BLK, HS), bf16),
            V((4, 2 * BLK, HS), bf16),
            V(block, bf16),
            V(block, bf16),
            V(block, bf16),
            V(block, bf16),
            V(block, bf16),
            V(block, bf16),
            V((NCH, 2, EXP, PACK, CW), bf16),
            V((NCH, 2, EXP, PACK, CW), bf16),
            V((TOK, D), bf16),
            V((TOK, D), bf16),
            V((TOK, D), f32),
            V((640, HS), bf16),
            V((2 * TOK, 256), bf16),
            V((4, 8, 384), f32),
            dma((2,)), dma((2,)), dma((2,)),
            dma((NCH,)), dma((NCH, 4, 2)), dma((NCH, 2, 4)),
            dma((3, NCH)), dma((3, NCH)),
            dma((4,)), dma((4,)), dma((4,)), dma((4,)),
            dma((3, NCH)), dma((3, NCH)),
            dma((NCH,)), dma((NCH, 4, 2)), dma((NCH, 2, 4)),
            dma((2, 2 * NCH)), dma((2, 2 * NCH)),
        ],
        compiler_params=pltpu.CompilerParams(
            collective_id=0, has_side_effects=True, vmem_limit_bytes=56 * 2**20
        ),
    )(fwd_act, fwd_ids, bwd_act, bwd_ids, bwd_grad, norm_gain, rt, w_gate[0], w_down[0], saved)


def solution(mesh):
    return jax.shard_map(
        on_device,
        mesh=mesh,
        in_specs=(
            P(("pp", "ep"), None),
            P(("pp", "ep"), None),
            P(("pp", "ep"), None),
            P(("pp", "ep"), None),
            P(("pp", "ep"), None),
            P("pp", None),
            P("pp", None, None),
            P(("pp", "ep"), None, None),
            P(("pp", "ep"), None, None),
            P("pp", "ep", None, None),
        ),
        out_specs=(P(("pp", "ep"), None), P(("pp", "ep"), None)),
        check_vma=False,
    )
```

```python
import functools

import jax
import jax.numpy as jnp
from jax import lax
from jax.experimental import pallas as pl
from jax.experimental.pallas import tpu as pltpu
from jax.sharding import PartitionSpec as P

MESH = pl.DeviceIdType.MESH
bf16 = jnp.bfloat16
f32 = jnp.float32
epsilon = 1e-06
route_scale = 2.5

TOK = 64
CAP = 17
EXP = 4
SUB = 256
PACK = 128
BLK = 144
HS = 128
MIRROR = (0, 2, 1, 3)
BWD, FWD = 0, 1


def plan(half):
    pieces = half // SUB
    if pieces == 7:
        return [(0, 32), (32, 32), (64, 32), (96, 32)], [(0, 1), (1, 3), (3, 5), (5, 7)], [(0, 2), (2, 4), (4, 6), (6, 7)]
    return [(0, 32), (32, 96)], [(0, 1), (1, pieces)], [(0, 2), (2, pieces)]


def iota(shape, dim):
    return lax.broadcasted_iota(jnp.int32, shape, dim)


def mm(a, b):
    return lax.dot_general(a, b, (((1,), (0,)), ((), ())), preferred_element_type=f32)


def mm_nt(a, b):
    return lax.dot_general(a, b, (((1,), (1,)), ((), ())), preferred_element_type=f32)


def select(mask):
    return mask.astype(f32).astype(bf16)


def group_of(q):
    return (q >= 17).astype(jnp.int32) + (q >= 34).astype(jnp.int32) + (q >= 51).astype(jnp.int32)


def kernel(
    fa_hbm, fid, ba_hbm, bid, bg_hbm, gain, rt, wg_hbm, wd_hbm, saved,
    fout, bout,
    fa, ba, bg,
    S, RY, A, WG, WD, zo, zs, zr, hx, o3, relay, o1, o2, fup, fdn, fin, TS, TR,
    fst, bst, gpre, svp, dots,
    ld, wl, wsend, wrecv, dloc, dsend, drecv, asend, arecv, zsend, zrecv, hsend, hrecv,
    rsend, rrecv, tloc, tsend, trecv, osend, orecv,
):
    D = fa.shape[1]
    n_saved = saved.shape[0]
    HF = D // 2
    NS = HF // SUB
    CUTS, OUT, BACK = plan(HF)
    NC = range(len(CUTS))
    n_pp = lax.axis_size("pp")
    pp = lax.axis_index("pp")
    ep = lax.axis_index("ep")
    y = ep // 8
    x = (ep // 2) % 4
    c = ep % 2

    def dev(yy, xx, cc):
        return (pp, (yy * 4 + xx) * 2 + cc)

    up = 1 + 2 * c
    x_up = (x + up) % 4
    x_dn = (x + 4 - up) % 4
    x_op = (x + 2) % 4
    d_up = dev(y, x_up, c)
    d_dn = dev(y, x_dn, c)
    d_sib = dev(y, x, 1 - c)
    d_zn = ((pp + 1) % n_pp, ep)
    d_zp = ((pp + n_pp - 1) % n_pp, ep)
    others = [(dy, dc) for dy in range(4) for dc in range(2) if (dy, dc) != (0, 0)]

    def remote(src, dst, ssem, rsem, device):
        return pltpu.make_async_remote_copy(
            src_ref=src, dst_ref=dst, send_sem=ssem, recv_sem=rsem, device_id=device, device_id_type=MESH
        )

    def arrive(buf, sem):
        remote(buf, buf, sem, sem, d_sib).wait_recv()

    barrier = pltpu.get_barrier_semaphore()
    partners = [dev((y + dy) % 4, x, (c + dc) % 2) for dy, dc in others] + [d_up, d_dn, d_zn, d_zp]
    for partner in partners:
        pl.semaphore_signal(barrier, inc=1, device_id=partner, device_id_type=MESH)

    mine = pl.multiple_of(c * HF, 128)
    yours = pl.multiple_of((1 - c) * HF, 128)
    own_w = [
        pltpu.make_async_copy(wg_hbm.at[pl.ds(mine, HF), :], WG.at[:, pl.ds(0, HS)], wl.at[0]),
        pltpu.make_async_copy(wd_hbm.at[:, pl.ds(mine, HF)], WD.at[pl.ds(0, HS), :], wl.at[1]),
    ]
    load_bg, load_fa, load_ba, load_saved = [
        pltpu.make_async_copy(bg_hbm, bg, ld.at[0]),
        pltpu.make_async_copy(fa_hbm, fa, ld.at[1]),
        pltpu.make_async_copy(ba_hbm, ba, ld.at[2]),
        pltpu.make_async_copy(saved, svp.at[pl.ds(0, n_saved)], ld.at[3]),
    ]
    for copy in [load_bg, load_fa] + own_w + [load_ba, load_saved]:
        copy.start()
    give_w = [
        remote(wg_hbm.at[pl.ds(yours, HF), :], WG.at[:, pl.ds(HS, HS)], wsend.at[0], wrecv.at[0], d_sib),
        remote(wd_hbm.at[:, pl.ds(yours, HF)], WD.at[pl.ds(HS, HS), :], wsend.at[1], wrecv.at[1], d_sib),
    ]

    def rows(ch):
        return pl.ds(*CUTS[ch])

    def part(cut):
        return pl.ds(cut[0] * SUB, (cut[1] - cut[0]) * SUB)

    def cols(c2, j):
        return slice(c2 * HF + j * SUB, c2 * HF + (j + 1) * SUB)

    def wide(c2, cut):
        return slice(c2 * HF + cut[0] * SUB, c2 * HF + cut[1] * SUB)

    every = [(c2, j) for j in range(NS) for c2 in range(2)]

    def row_of(j):
        return 1 + 17 * j

    def pieces_in(ch):
        lo, n = CUTS[ch]
        return [j for j in range(NS) if row_of(j) < lo + n and row_of(j) + 17 > lo]

    def span(j):
        hold = [cut for ch, cut in enumerate(CUTS) if j in pieces_in(ch)]
        return hold[0][0], hold[-1][0] + hold[-1][1]

    def inverse(h_ref):
        total = jnp.zeros((TOK, SUB), f32)
        for at in every:
            v = h_ref[:, cols(*at)].astype(f32)
            total = total + v * v
        return lax.rsqrt(jnp.sum(total, axis=-1, keepdims=True) * (1.0 / D) + epsilon)

    def normed(h_ref, inv, at):
        return (h_ref[:, cols(*at)].astype(f32) * inv * gain[:, cols(*at)].astype(f32)).astype(bf16)

    before = select(iota((TOK, TOK), 0) < iota((TOK, TOK), 1))
    eye = select(iota((TOK, TOK), 0) == iota((TOK, TOK), 1))

    def routes(id_ref):
        ids = id_ref[...]
        onehot = (iota((16, TOK), 0) == ids).astype(f32)
        earlier = mm(onehot.astype(bf16), before)
        place = jnp.sum(onehot * earlier, axis=0, keepdims=True)
        return onehot, place, ids.astype(f32)

    def columns(onehot, place, ids):
        line = iota((16, TOK), 0)
        both = jnp.where(line == 0, ids, jnp.where(line == 1, place, 0.0))
        turned = mm_nt(eye, both.astype(bf16))
        one = mm_nt(eye, onehot.astype(bf16))[:, :EXP]
        return one, turned[:, 1:2], turned[:, 0:1]

    def send_desc(m, ch, dy, dc):
        e, c2 = (y + dy) % 4, (c + dc) % 2
        return remote(
            S.at[m, c2, e, rows(ch)], RY.at[m, c, y, rows(ch)],
            dsend.at[m, ch, dy, dc], drecv.at[m, ch, c, y], dev(e, x, c2),
        )

    def keep_desc(m, ch):
        return pltpu.make_async_copy(S.at[m, c, y, rows(ch)], RY.at[m, c, y, rows(ch)], dloc.at[m, ch])

    def dispatch(m, ch, table, token_rows):
        lo, n = CUTS[ch]
        k = iota((EXP * n, 1), 0)
        k = (k + (PACK - n) * (k // n) + lo).astype(f32)
        picks = [(j, select(k == table[2] * PACK + (table[1] + row_of(j)))) for j in pieces_in(ch)]
        for c2 in range(2):
            filled = jnp.zeros((EXP * n, SUB), f32)
            for j, pick in picks:
                filled = filled + mm(pick, token_rows(c2, j))
            S[m, c2, :, rows(ch)] = filled.astype(bf16).reshape(EXP, n, SUB)
        if (m, ch) == (BWD, 0):
            pl.semaphore_wait(barrier, len(partners))
        for dy, dc in others:
            send_desc(m, ch, dy, dc).start()
        keep_desc(m, ch).start()

    b_routes = routes(bid)
    load_bg.wait()
    for ch in NC:
        dispatch(BWD, ch, b_routes, lambda c2, j: bg[:, cols(c2, j)])
    for copy in give_w:
        copy.start()

    r = iota((BLK, 1), 0)
    core = (r >= 68).astype(jnp.int32)
    q = r - 68 * core
    q_y = group_of(q)

    def compact(j):
        lo, hi = span(j)
        want = jnp.where(r < 136, (core * 4 + q_y) * (hi - lo) + (q - 17 * q_y) + (row_of(j) - lo), -1)
        return select(want == iota((BLK, 8 * (hi - lo)), 1))

    def ag_own(m, ch):
        at = part(OUT[ch])
        src = A.at[m, 0, :, at]
        return [
            remote(src, A.at[m, 1, :, at], asend.at[m, 0, ch], arecv.at[m, 0, ch], d_up),
            remote(src, A.at[m, 2, :, at], asend.at[m, 1, ch], arecv.at[m, 1, ch], d_dn),
        ]

    def ag_on(m, ch):
        at = part(OUT[ch])
        return remote(A.at[m, 1, :, at], A.at[m, 3, :, at], asend.at[m, 2, ch], arecv.at[m, 2, ch], d_up)

    def gather(m, ch):
        for dy, dc in others:
            sy, sc = (y + dy) % 4, (c + dc) % 2
            arrive(RY.at[m, sc, sy, rows(ch)], drecv.at[m, ch, sc, sy])
        keep_desc(m, ch).wait()
        for j in range(*OUT[ch]):
            lo, hi = span(j)
            packs = RY[m, :, :, lo:hi].reshape(8 * (hi - lo), SUB)
            A[m, 0, :, j * SUB : (j + 1) * SUB] = mm(compact(j), packs).astype(bf16)
        for copy in ag_own(m, ch):
            copy.start()

    def pass_on(m, ch):
        arrive(A.at[m, 1, :, part(OUT[ch])], arecv.at[m, 0, ch])
        ag_on(m, ch).start()

    def have(m, slot):
        for ch in NC:
            arrive(A.at[m, slot, :, part(OUT[ch])], arecv.at[m, slot - 1, ch])

    def z_copy(m, s):
        o = MIRROR[s]
        return remote(zs.at[m, s], zr.at[m, o], zsend.at[m, s], zrecv.at[m, o], d_sib)

    def h_copy(m, s):
        o = MIRROR[s]
        return remote(
            hx.at[m, s, :, pl.ds(0, HS)], hx.at[m, o, :, pl.ds(HS, HS)], hsend.at[m, s], hrecv.at[m, o], d_sib
        )

    def project(m, s):
        z = mm(A[m, s], WG[...]) if m == FWD else mm_nt(A[m, s], WD[...])
        zo[m, s] = z[:, :HS]
        zs[m, s] = z[:, HS:]
        z_copy(m, s).start()

    saved_at = jnp.where(r < 136, q + 119 * q_y + 17 * core, -100000)

    def activate(m, s, xs):
        arrive(zr.at[m, s], zrecv.at[m, s])
        z = zo[m, s] + zr[m, s]
        if m == FWD:
            hx[m, s, :, :HS] = (z * jax.nn.sigmoid(z)).astype(bf16)
            h_copy(m, s).start()
            return
        sv = mm(select(iota((BLK, svp.shape[0]), 1) - 34 * xs == saved_at), svp[...])
        sig = jax.nn.sigmoid(sv)
        hx[m, s, :, :HS] = (z * sig * (1.0 + sv * (1.0 - sig))).astype(bf16)
        h_copy(m, s).start()
        prod = (sv * sig).astype(bf16).astype(f32) * z
        prod = jnp.concatenate([prod, jnp.zeros((256 - BLK, HS), f32)], axis=0)
        dots[s] = lax.dot_general(
            jnp.ones((8, HS), f32), prod, (((1,), (1,)), ((), ())),
            preferred_element_type=f32, precision=lax.Precision.HIGHEST,
        )

    def ready(m, s):
        arrive(hx.at[m, s, :, pl.ds(HS, HS)], hrecv.at[m, s])

    def produce(m, s, ch):
        lo, w = BACK[ch][0] * SUB, (BACK[ch][1] - BACK[ch][0]) * SUB
        if m == FWD:
            return mm(hx[m, s], WD[:, lo : lo + w])
        out = mm_nt(hx[m, s], WG[lo : lo + w, :])
        if ch == 0:
            spare = dots[s]
            if w > 256:
                spare = jnp.concatenate([spare, jnp.zeros((8, w - 256), f32)], axis=1)
            out = jnp.concatenate([out[:136], spare], axis=0)
        return out

    def leg(k, src, dst, device):
        def copy(m, ch):
            at = part(BACK[ch])
            return remote(src.at[m, :, at], dst.at[m, :, at], rsend.at[m, k, ch], rrecv.at[m, k, ch], device)

        return copy

    down3 = leg(0, o3, relay, d_dn)
    down1 = leg(1, o1, fup, d_dn)
    up2 = leg(2, o2, fdn, d_up)

    def give2(m, ch):
        o2[m, :, part(BACK[ch])] = produce(m, 2, ch).astype(bf16)
        up2(m, ch).start()

    def give3(m, ch):
        o3[m, :, part(BACK[ch])] = produce(m, 3, ch).astype(bf16)
        down3(m, ch).start()

    def give1(m, ch):
        at = part(BACK[ch])
        own = produce(m, 1, ch)
        arrive(relay.at[m, :, at], rrecv.at[m, 0, ch])
        o1[m, :, at] = (own + relay[m, :, at].astype(f32)).astype(bf16)
        down1(m, ch).start()

    def back_desc(m, ch, dy, dc):
        ty, tc = (y + dy) % 4, (c + dc) % 2
        return remote(
            TS.at[m, tc, ty, rows(ch)], TR.at[m, c, y, rows(ch)],
            tsend.at[m, ch, dy, dc], trecv.at[m, ch, c, y], dev(ty, x, tc),
        )

    def stay_desc(m, ch):
        return pltpu.make_async_copy(TS.at[m, c, y, rows(ch)], TR.at[m, c, y, rows(ch)], tloc.at[m, ch])

    def give0(m, ch):
        at = part(BACK[ch])
        out = produce(m, 0, ch)
        arrive(fdn.at[m, :, at], rrecv.at[m, 2, ch])
        out = out + fdn[m, :, at].astype(f32)
        arrive(fup.at[m, :, at], rrecv.at[m, 1, ch])
        fin[m, :, at] = (out + fup[m, :, at].astype(f32)).astype(bf16)
        lo, n = CUTS[ch]
        k = iota((8 * n, 1), 0)
        owner = k // n
        g = k - n * owner + lo
        filled = jnp.zeros((8 * n, SUB), f32)
        for j in pieces_in(ch):
            first = row_of(j)
            source = jnp.where((g >= first) & (g < first + 17), 17 * owner + g - first, -1)
            if m == BWD and j == 0:
                source = jnp.where(g == 0, 136, source)
            filled = filled + mm(select(source == iota((8 * n, BLK), 1)), fin[m, :, j * SUB : (j + 1) * SUB])
        TS[m, :, :, rows(ch)] = filled.astype(bf16).reshape(2, EXP, n, SUB)
        for dy, dc in others:
            back_desc(m, ch, dy, dc).start()
        stay_desc(m, ch).start()

    def returned(m, ch):
        for dy, dc in others:
            ey, hc = (y + dy) % 4, (c + dc) % 2
            arrive(TR.at[m, hc, ey, rows(ch)], trecv.at[m, ch, hc, ey])
        stay_desc(m, ch).wait()

    def rows_of(m, table, at):
        c2, j = at
        lo, hi = span(j)
        spot = table[2] * (hi - lo) + (table[1] + (row_of(j) - lo))
        spots = select(spot == iota((TOK, EXP * (hi - lo)), 1).astype(f32))
        return mm(spots, TR[m, c2, :, lo:hi].reshape(EXP * (hi - lo), SUB))

    def fwd_copy(c2, ch):
        at = wide(c2, OUT[ch])
        return remote(fst.at[:, at], fout.at[:, at], osend.at[1, c2, ch], orecv.at[1, c2, ch], d_zn)

    def bwd_copy(c2, ch):
        at = wide(c2, OUT[ch])
        return remote(bst.at[:, at], bout.at[:, at], osend.at[0, c2, ch], orecv.at[0, c2, ch], d_zp)

    for ch in NC:
        gather(BWD, ch)
    f_routes = routes(fid)
    load_fa.wait()
    f_inv = inverse(fa)
    for at in every:
        fst[:, cols(*at)] = normed(fa, f_inv, at)
    for ch in NC:
        dispatch(FWD, ch, f_routes, lambda c2, j: fst[:, cols(c2, j)])
    for ch in NC:
        pass_on(BWD, ch)
        gather(FWD, ch)

    f_table = columns(*f_routes)
    b_table = columns(*b_routes)
    b_one, b_place = b_table[:2]
    f_aff = jax.nn.sigmoid(mm_nt(fst[...], rt[...]))
    f_gate = jnp.sum(f_table[0] * f_aff, axis=-1, keepdims=True)
    load_ba.wait()
    load_saved.wait()
    svp[n_saved:] = jnp.zeros((svp.shape[0] - n_saved, HS), bf16)
    for copy in own_w:
        copy.wait()
    arrive(WG.at[:, pl.ds(HS, HS)], wrecv.at[0])
    arrive(WD.at[pl.ds(HS, HS), :], wrecv.at[1])
    project(BWD, 0)
    project(BWD, 1)
    b_inv = inverse(ba)
    for at in every:
        bst[:, cols(*at)] = normed(ba, b_inv, at)
    b_aff = jax.nn.sigmoid(mm_nt(bst[...], rt[...]))
    b_gate = jnp.sum(b_one * b_aff, axis=-1, keepdims=True)
    pass_on(FWD, 0)
    have(BWD, 2)
    project(BWD, 2)
    activate(BWD, 0, x)
    activate(BWD, 1, x_dn)
    activate(BWD, 2, x_up)
    for ch in NC[1:]:
        pass_on(FWD, ch)
    project(FWD, 0)
    project(FWD, 1)
    ready(BWD, 2)
    for ch in NC:
        give2(BWD, ch)
    have(BWD, 3)
    project(BWD, 3)
    activate(FWD, 0, x)
    activate(BWD, 3, x_op)
    ready(BWD, 3)
    for ch in NC:
        give3(BWD, ch)
    have(FWD, 2)
    project(FWD, 2)
    activate(FWD, 1, x_dn)
    activate(FWD, 2, x_up)
    ready(BWD, 1)
    for ch in NC:
        give1(BWD, ch)
    have(FWD, 3)
    project(FWD, 3)
    activate(FWD, 3, x_op)
    ready(FWD, 2)
    ready(FWD, 3)
    n = len(NC)
    for ch in NC[: min(3, n)]:
        give3(FWD, ch)
    for ch in NC[: min(2, n)]:
        give2(FWD, ch)
    ready(BWD, 0)
    for ch in NC:
        give0(BWD, ch)
    ready(FWD, 1)
    ready(FWD, 0)
    mean = jnp.zeros((TOK, SUB), f32)
    grad_logits = None
    for ch in NC:
        give1(FWD, ch)
        if ch + 3 < n:
            give3(FWD, ch + 3)
        if ch + 2 < n:
            give2(FWD, ch + 2)
        returned(BWD, ch)
        if ch == 0:
            hit = (68 * c + 17 * y).astype(f32) + b_place == iota((TOK, SUB), 1).astype(f32)
            dot = jnp.zeros((TOK, 1), f32)
            for e in range(EXP):
                both = TR[BWD, 0, e, 0:16].astype(f32) + TR[BWD, 1, e, 0:16].astype(f32)
                found = jnp.sum(jnp.where(hit, both[0:1, :], 0.0), axis=-1, keepdims=True)
                dot = dot + b_one[:, e : e + 1] * found
            grad_aff = b_one * (route_scale * dot)
            grad_logits = (grad_aff * b_aff * (1.0 - b_aff)).astype(bf16)
        for at in [(c2, j) for j in range(*OUT[ch]) for c2 in range(2)]:
            grad_n = (route_scale * b_gate) * rows_of(BWD, b_table, at) + mm(grad_logits, rt[:, cols(*at)])
            pre = grad_n * gain[:, cols(*at)].astype(f32)
            gpre[:, cols(*at)] = pre
            mean = mean + pre * ba[:, cols(*at)].astype(f32)
        if ch >= 2:
            give0(FWD, ch - 2)
    factor = b_inv * b_inv * (jnp.sum(mean, axis=-1, keepdims=True) * (1.0 / D))
    for ch in NC:
        for c2 in range(2):
            at = wide(c2, OUT[ch])
            grad = b_inv * (gpre[:, at] - ba[:, at].astype(f32) * factor)
            bst[:, at] = (bg[:, at].astype(f32) + grad).astype(bf16)
            bwd_copy(c2, ch).start()

    def finish_fwd(ch):
        returned(FWD, ch)
        for c2 in range(2):
            for j in range(*OUT[ch]):
                at = cols(c2, j)
                fst[:, at] = (
                    fa[:, at].astype(f32) + route_scale * (f_gate * rows_of(FWD, f_table, (c2, j)))
                ).astype(bf16)
            fwd_copy(c2, ch).start()

    for ch in range(n - 2, n):
        if ch - 2 >= 0:
            finish_fwd(ch - 2)
        give0(FWD, ch)
    for ch in range(max(n - 2, 0), n):
        finish_fwd(ch)

    for copy in give_w:
        copy.wait_send()
    for m in (BWD, FWD):
        for ch in NC:
            for dy, dc in others:
                send_desc(m, ch, dy, dc).wait_send()
                back_desc(m, ch, dy, dc).wait_send()
            for copy in ag_own(m, ch) + [ag_on(m, ch), down3(m, ch), down1(m, ch), up2(m, ch)]:
                copy.wait_send()
        for s in range(4):
            z_copy(m, s).wait_send()
            h_copy(m, s).wait_send()
    for ch in NC:
        for c2 in range(2):
            fwd_copy(c2, ch).wait()
            bwd_copy(c2, ch).wait()


def on_device(
    fwd_act, fwd_ids, bwd_act, bwd_ids, bwd_grad, norm_gain, router, w_gate, w_down, saved_gate
):
    D = fwd_act.shape[1]
    HF = D // 2
    n = len(plan(HF)[0])
    saved = saved_gate[0, 0]
    vmem = pl.BlockSpec(memory_space=pltpu.VMEM)
    hbm = pl.BlockSpec(memory_space=pl.ANY)
    dma = pltpu.SemaphoreType.DMA
    V = pltpu.VMEM
    packs = V((2, 2, EXP, PACK, SUB), bf16)
    sums = V((2, BLK, HF), bf16)
    return pl.pallas_call(
        kernel,
        out_shape=[jax.ShapeDtypeStruct((TOK, D), bf16)] * 2,
        in_specs=[hbm, vmem, hbm, vmem, hbm, vmem, vmem] + [hbm] * 3,
        out_specs=[hbm, hbm],
        scratch_shapes=[
            V((TOK, D), bf16),
            V((TOK, D), bf16),
            V((TOK, D), bf16),
            packs,
            packs,
            V((2, 4, BLK, HF), bf16),
            V((HF, 2 * HS), bf16),
            V((2 * HS, HF), bf16),
            V((2, 4, BLK, HS), f32),
            V((2, 4, BLK, HS), f32),
            V((2, 4, BLK, HS), f32),
            V((2, 4, BLK, 2 * HS), bf16),
            sums, sums, sums, sums, sums, sums, sums,
            packs,
            packs,
            V((TOK, D), bf16),
            V((TOK, D), bf16),
            V((TOK, D), f32),
            V((640, HS), bf16),
            V((4, 8, 256), f32),
            dma((4,)), dma((2,)), dma((2,)), dma((2,)),
            dma((2, n)), dma((2, n, 4, 2)), dma((2, n, 2, 4)),
            dma((2, 3, n)), dma((2, 3, n)),
            dma((2, 4)), dma((2, 4)), dma((2, 4)), dma((2, 4)),
            dma((2, 3, n)), dma((2, 3, n)),
            dma((2, n)), dma((2, n, 4, 2)), dma((2, n, 2, 4)),
            dma((2, 2, n)), dma((2, 2, n)),
        ],
        compiler_params=pltpu.CompilerParams(
            collective_id=0, has_side_effects=True, vmem_limit_bytes=56 * 2**20
        ),
    )(
        fwd_act, fwd_ids.reshape(1, TOK), bwd_act, bwd_ids.reshape(1, TOK), bwd_grad, norm_gain,
        router[0].T, w_gate[0], w_down[0], saved,
    )


def solution(mesh):
    return jax.shard_map(
        on_device,
        mesh=mesh,
        in_specs=(
            P(("pp", "ep"), None),
            P(("pp", "ep"), None),
            P(("pp", "ep"), None),
            P(("pp", "ep"), None),
            P(("pp", "ep"), None),
            P("pp", None),
            P("pp", None, None),
            P(("pp", "ep"), None, None),
            P(("pp", "ep"), None, None),
            P("pp", "ep", None, None),
        ),
        out_specs=(P(("pp", "ep"), None), P(("pp", "ep"), None)),
        check_vma=False,
    )
```

```python
import functools

import jax
import jax.numpy as jnp
from jax import lax
from jax.experimental import pallas as pl
from jax.experimental.pallas import tpu as pltpu
from jax.sharding import PartitionSpec as P

MESH = pl.DeviceIdType.MESH
bf16 = jnp.bfloat16
f32 = jnp.float32
epsilon = 1e-06
route_scale = 2.5

TOK = 64
CAP = 17
EXP = 4
SUB = 256
PACK = 128
BLK = 144
HS = 128
MIRROR = (0, 2, 1, 3)
BWD, FWD = 0, 1


def plan(half):
    pieces = half // SUB
    if pieces == 7:
        return [(0, 32), (32, 32), (64, 32), (96, 32)], [(0, 1), (1, 3), (3, 5), (5, 7)], [(0, 2), (2, 4), (4, 6), (6, 7)]
    return [(0, 32), (32, 96)], [(0, 1), (1, pieces)], [(0, 2), (2, pieces)]


def iota(shape, dim):
    return lax.broadcasted_iota(jnp.int32, shape, dim)


def mm(a, b):
    return lax.dot_general(a, b, (((1,), (0,)), ((), ())), preferred_element_type=f32)


def mm_nt(a, b):
    return lax.dot_general(a, b, (((1,), (1,)), ((), ())), preferred_element_type=f32)


def select(mask):
    return mask.astype(f32).astype(bf16)


def group_of(q):
    return (q >= 17).astype(jnp.int32) + (q >= 34).astype(jnp.int32) + (q >= 51).astype(jnp.int32)


def kernel(
    fa_hbm, fid, ba_hbm, bid, bg_hbm, gain, rt, wg_hbm, wd_hbm, saved,
    fout, bout,
    fa, ba, bg,
    S, RY, A, WG, WD, zo, zs, zr, hx, o3, relay, o1, o2, fup, fdn, fin, TS, TR,
    fst, bst, gpre, svp, dots,
    ld, wl, wsend, wrecv, dloc, dsend, drecv, asend, arecv, zsend, zrecv, hsend, hrecv,
    rsend, rrecv, tloc, tsend, trecv, osend, orecv,
):
    D = fa.shape[1]
    n_saved = saved.shape[0]
    HF = D // 2
    NS = HF // SUB
    CUTS, OUT, BACK = plan(HF)
    NC = range(len(CUTS))
    n_pp = lax.axis_size("pp")
    pp = lax.axis_index("pp")
    ep = lax.axis_index("ep")
    y = ep // 8
    x = (ep // 2) % 4
    c = ep % 2

    def dev(yy, xx, cc):
        return (pp, (yy * 4 + xx) * 2 + cc)

    up = 1 + 2 * c
    x_up = (x + up) % 4
    x_dn = (x + 4 - up) % 4
    x_op = (x + 2) % 4
    d_up = dev(y, x_up, c)
    d_dn = dev(y, x_dn, c)
    d_sib = dev(y, x, 1 - c)
    d_zn = ((pp + 1) % n_pp, ep)
    d_zp = ((pp + n_pp - 1) % n_pp, ep)
    others = [(2, 0), (2, 1), (1, 0), (3, 0), (1, 1), (3, 1), (0, 1)]

    def remote(src, dst, ssem, rsem, device):
        return pltpu.make_async_remote_copy(
            src_ref=src, dst_ref=dst, send_sem=ssem, recv_sem=rsem, device_id=device, device_id_type=MESH
        )

    def arrive(buf, sem):
        remote(buf, buf, sem, sem, d_sib).wait_recv()

    barrier = pltpu.get_barrier_semaphore()
    partners = [dev((y + dy) % 4, x, (c + dc) % 2) for dy, dc in others] + [d_up, d_dn, d_zn, d_zp]
    for partner in partners:
        pl.semaphore_signal(barrier, inc=1, device_id=partner, device_id_type=MESH)

    mine = pl.multiple_of(c * HF, 128)
    yours = pl.multiple_of((1 - c) * HF, 128)
    own_w = [
        pltpu.make_async_copy(wg_hbm.at[pl.ds(mine, HF), :], WG.at[:, pl.ds(0, HS)], wl.at[0]),
        pltpu.make_async_copy(wd_hbm.at[:, pl.ds(mine, HF)], WD.at[pl.ds(0, HS), :], wl.at[1]),
    ]
    load_bg, load_fa, load_ba, load_saved = [
        pltpu.make_async_copy(bg_hbm, bg, ld.at[0]),
        pltpu.make_async_copy(fa_hbm, fa, ld.at[1]),
        pltpu.make_async_copy(ba_hbm, ba, ld.at[2]),
        pltpu.make_async_copy(saved, svp.at[pl.ds(0, n_saved)], ld.at[3]),
    ]
    for copy in [load_bg, load_fa] + own_w + [load_ba, load_saved]:
        copy.start()
    give_w = [
        remote(wg_hbm.at[pl.ds(yours, HF), :], WG.at[:, pl.ds(HS, HS)], wsend.at[0], wrecv.at[0], d_sib),
        remote(wd_hbm.at[:, pl.ds(yours, HF)], WD.at[pl.ds(HS, HS), :], wsend.at[1], wrecv.at[1], d_sib),
    ]

    def rows(ch):
        return pl.ds(*CUTS[ch])

    def part(cut):
        return pl.ds(cut[0] * SUB, (cut[1] - cut[0]) * SUB)

    def cols(c2, j):
        return slice(c2 * HF + j * SUB, c2 * HF + (j + 1) * SUB)

    def wide(c2, cut):
        return slice(c2 * HF + cut[0] * SUB, c2 * HF + cut[1] * SUB)

    every = [(c2, j) for j in range(NS) for c2 in range(2)]

    def row_of(j):
        return 1 + 17 * j

    def pieces_in(ch):
        lo, n = CUTS[ch]
        return [j for j in range(NS) if row_of(j) < lo + n and row_of(j) + 17 > lo]

    def span(j):
        hold = [cut for ch, cut in enumerate(CUTS) if j in pieces_in(ch)]
        return hold[0][0], hold[-1][0] + hold[-1][1]

    def inverse(h_ref):
        total = jnp.zeros((TOK, SUB), f32)
        for at in every:
            v = h_ref[:, cols(*at)].astype(f32)
            total = total + v * v
        return lax.rsqrt(jnp.sum(total, axis=-1, keepdims=True) * (1.0 / D) + epsilon)

    def normed(h_ref, inv, at):
        return (h_ref[:, cols(*at)].astype(f32) * inv * gain[:, cols(*at)].astype(f32)).astype(bf16)

    before = select(iota((TOK, TOK), 0) < iota((TOK, TOK), 1))
    eye = select(iota((TOK, TOK), 0) == iota((TOK, TOK), 1))

    def routes(id_ref):
        ids = id_ref[...]
        onehot = (iota((16, TOK), 0) == ids).astype(f32)
        earlier = mm(onehot.astype(bf16), before)
        place = jnp.sum(onehot * earlier, axis=0, keepdims=True)
        return onehot, place, ids.astype(f32)

    def columns(onehot, place, ids):
        line = iota((16, TOK), 0)
        both = jnp.where(line == 0, ids, jnp.where(line == 1, place, 0.0))
        turned = mm_nt(eye, both.astype(bf16))
        one = mm_nt(eye, onehot.astype(bf16))[:, :EXP]
        return one, turned[:, 1:2], turned[:, 0:1]

    def send_desc(m, ch, dy, dc):
        e, c2 = (y + dy) % 4, (c + dc) % 2
        return remote(
            S.at[m, c2, e, rows(ch)], RY.at[m, c, y, rows(ch)],
            dsend.at[m, ch, dy, dc], drecv.at[m, ch, c, y], dev(e, x, c2),
        )

    def keep_desc(m, ch):
        return pltpu.make_async_copy(S.at[m, c, y, rows(ch)], RY.at[m, c, y, rows(ch)], dloc.at[m, ch])

    def dispatch(m, ch, table, token_rows):
        lo, n = CUTS[ch]
        k = iota((EXP * n, 1), 0)
        k = (k + (PACK - n) * (k // n) + lo).astype(f32)
        picks = [(j, select(k == table[2] * PACK + (table[1] + row_of(j)))) for j in pieces_in(ch)]
        for c2 in range(2):
            filled = jnp.zeros((EXP * n, SUB), f32)
            for j, pick in picks:
                filled = filled + mm(pick, token_rows(c2, j))
            S[m, c2, :, rows(ch)] = filled.astype(bf16).reshape(EXP, n, SUB)
        if (m, ch) == (BWD, 0):
            pl.semaphore_wait(barrier, len(partners))
        for dy, dc in others:
            send_desc(m, ch, dy, dc).start()
        keep_desc(m, ch).start()

    b_routes = routes(bid)
    load_bg.wait()
    for ch in NC:
        dispatch(BWD, ch, b_routes, lambda c2, j: bg[:, cols(c2, j)])
    for copy in give_w:
        copy.start()

    r = iota((BLK, 1), 0)
    core = (r >= 68).astype(jnp.int32)
    q = r - 68 * core
    q_y = group_of(q)

    def compact(j):
        lo, hi = span(j)
        want = jnp.where(r < 136, (core * 4 + q_y) * (hi - lo) + (q - 17 * q_y) + (row_of(j) - lo), -1)
        return select(want == iota((BLK, 8 * (hi - lo)), 1))

    def ag_own(m, ch):
        at = part(OUT[ch])
        src = A.at[m, 0, :, at]
        return [
            remote(src, A.at[m, 1, :, at], asend.at[m, 0, ch], arecv.at[m, 0, ch], d_up),
            remote(src, A.at[m, 2, :, at], asend.at[m, 1, ch], arecv.at[m, 1, ch], d_dn),
        ]

    def ag_on(m, ch):
        at = part(OUT[ch])
        return remote(A.at[m, 1, :, at], A.at[m, 3, :, at], asend.at[m, 2, ch], arecv.at[m, 2, ch], d_up)

    def gather(m, ch):
        for dy, dc in others:
            sy, sc = (y + dy) % 4, (c + dc) % 2
            arrive(RY.at[m, sc, sy, rows(ch)], drecv.at[m, ch, sc, sy])
        keep_desc(m, ch).wait()
        for j in range(*OUT[ch]):
            lo, hi = span(j)
            packs = RY[m, :, :, lo:hi].reshape(8 * (hi - lo), SUB)
            A[m, 0, :, j * SUB : (j + 1) * SUB] = mm(compact(j), packs).astype(bf16)
        for copy in ag_own(m, ch):
            copy.start()

    def pass_on(m, ch):
        arrive(A.at[m, 1, :, part(OUT[ch])], arecv.at[m, 0, ch])
        ag_on(m, ch).start()

    def have(m, slot):
        for ch in NC:
            arrive(A.at[m, slot, :, part(OUT[ch])], arecv.at[m, slot - 1, ch])

    def z_copy(m, s):
        o = MIRROR[s]
        return remote(zs.at[m, s], zr.at[m, o], zsend.at[m, s], zrecv.at[m, o], d_sib)

    def h_copy(m, s):
        o = MIRROR[s]
        return remote(
            hx.at[m, s, :, pl.ds(0, HS)], hx.at[m, o, :, pl.ds(HS, HS)], hsend.at[m, s], hrecv.at[m, o], d_sib
        )

    def project(m, s):
        z = mm(A[m, s], WG[...]) if m == FWD else mm_nt(A[m, s], WD[...])
        zo[m, s] = z[:, :HS]
        zs[m, s] = z[:, HS:]
        z_copy(m, s).start()

    saved_at = jnp.where(r < 136, q + 119 * q_y + 17 * core, -100000)

    def activate(m, s, xs):
        arrive(zr.at[m, s], zrecv.at[m, s])
        z = zo[m, s] + zr[m, s]
        if m == FWD:
            hx[m, s, :, :HS] = (z * jax.nn.sigmoid(z)).astype(bf16)
            h_copy(m, s).start()
            return
        sv = mm(select(iota((BLK, svp.shape[0]), 1) - 34 * xs == saved_at), svp[...])
        sig = jax.nn.sigmoid(sv)
        hx[m, s, :, :HS] = (z * sig * (1.0 + sv * (1.0 - sig))).astype(bf16)
        h_copy(m, s).start()
        prod = (sv * sig).astype(bf16).astype(f32) * z
        prod = jnp.concatenate([prod, jnp.zeros((256 - BLK, HS), f32)], axis=0)
        dots[s] = lax.dot_general(
            jnp.ones((8, HS), f32), prod, (((1,), (1,)), ((), ())),
            preferred_element_type=f32, precision=lax.Precision.HIGHEST,
        )

    def ready(m, s):
        arrive(hx.at[m, s, :, pl.ds(HS, HS)], hrecv.at[m, s])

    def produce(m, s, ch):
        lo, w = BACK[ch][0] * SUB, (BACK[ch][1] - BACK[ch][0]) * SUB
        if m == FWD:
            return mm(hx[m, s], WD[:, lo : lo + w])
        out = mm_nt(hx[m, s], WG[lo : lo + w, :])
        if ch == 0:
            spare = dots[s]
            if w > 256:
                spare = jnp.concatenate([spare, jnp.zeros((8, w - 256), f32)], axis=1)
            out = jnp.concatenate([out[:136], spare], axis=0)
        return out

    def leg(k, src, dst, device):
        def copy(m, ch):
            at = part(BACK[ch])
            return remote(src.at[m, :, at], dst.at[m, :, at], rsend.at[m, k, ch], rrecv.at[m, k, ch], device)

        return copy

    down3 = leg(0, o3, relay, d_dn)
    down1 = leg(1, o1, fup, d_dn)
    up2 = leg(2, o2, fdn, d_up)

    def give2(m, ch):
        o2[m, :, part(BACK[ch])] = produce(m, 2, ch).astype(bf16)
        up2(m, ch).start()

    def give3(m, ch):
        o3[m, :, part(BACK[ch])] = produce(m, 3, ch).astype(bf16)
        down3(m, ch).start()

    def give1(m, ch):
        at = part(BACK[ch])
        own = produce(m, 1, ch)
        arrive(relay.at[m, :, at], rrecv.at[m, 0, ch])
        o1[m, :, at] = (own + relay[m, :, at].astype(f32)).astype(bf16)
        down1(m, ch).start()

    def back_desc(m, ch, dy, dc):
        ty, tc = (y + dy) % 4, (c + dc) % 2
        return remote(
            TS.at[m, tc, ty, rows(ch)], TR.at[m, c, y, rows(ch)],
            tsend.at[m, ch, dy, dc], trecv.at[m, ch, c, y], dev(ty, x, tc),
        )

    def stay_desc(m, ch):
        return pltpu.make_async_copy(TS.at[m, c, y, rows(ch)], TR.at[m, c, y, rows(ch)], tloc.at[m, ch])

    def give0(m, ch):
        at = part(BACK[ch])
        out = produce(m, 0, ch)
        arrive(fdn.at[m, :, at], rrecv.at[m, 2, ch])
        out = out + fdn[m, :, at].astype(f32)
        arrive(fup.at[m, :, at], rrecv.at[m, 1, ch])
        fin[m, :, at] = (out + fup[m, :, at].astype(f32)).astype(bf16)
        lo, n = CUTS[ch]
        k = iota((8 * n, 1), 0)
        owner = k // n
        g = k - n * owner + lo
        filled = jnp.zeros((8 * n, SUB), f32)
        for j in pieces_in(ch):
            first = row_of(j)
            source = jnp.where((g >= first) & (g < first + 17), 17 * owner + g - first, -1)
            if m == BWD and j == 0:
                source = jnp.where(g == 0, 136, source)
            filled = filled + mm(select(source == iota((8 * n, BLK), 1)), fin[m, :, j * SUB : (j + 1) * SUB])
        TS[m, :, :, rows(ch)] = filled.astype(bf16).reshape(2, EXP, n, SUB)
        for dy, dc in others:
            back_desc(m, ch, dy, dc).start()
        stay_desc(m, ch).start()

    def returned(m, ch):
        for dy, dc in others:
            ey, hc = (y + dy) % 4, (c + dc) % 2
            arrive(TR.at[m, hc, ey, rows(ch)], trecv.at[m, ch, hc, ey])
        stay_desc(m, ch).wait()

    def rows_of(m, table, at):
        c2, j = at
        lo, hi = span(j)
        spot = table[2] * (hi - lo) + (table[1] + (row_of(j) - lo))
        spots = select(spot == iota((TOK, EXP * (hi - lo)), 1).astype(f32))
        return mm(spots, TR[m, c2, :, lo:hi].reshape(EXP * (hi - lo), SUB))

    def fwd_copy(c2, ch):
        at = wide(c2, OUT[ch])
        return remote(fst.at[:, at], fout.at[:, at], osend.at[1, c2, ch], orecv.at[1, c2, ch], d_zn)

    def bwd_copy(c2, ch):
        at = wide(c2, OUT[ch])
        return remote(bst.at[:, at], bout.at[:, at], osend.at[0, c2, ch], orecv.at[0, c2, ch], d_zp)

    for ch in NC:
        gather(BWD, ch)
    f_routes = routes(fid)
    load_fa.wait()
    f_inv = inverse(fa)
    for at in every:
        fst[:, cols(*at)] = normed(fa, f_inv, at)
    for ch in NC:
        dispatch(FWD, ch, f_routes, lambda c2, j: fst[:, cols(c2, j)])
    for ch in NC:
        pass_on(BWD, ch)
        gather(FWD, ch)

    f_table = columns(*f_routes)
    b_table = columns(*b_routes)
    b_one, b_place = b_table[:2]
    f_aff = jax.nn.sigmoid(mm_nt(fst[...], rt[...]))
    f_gate = jnp.sum(f_table[0] * f_aff, axis=-1, keepdims=True)
    load_ba.wait()
    load_saved.wait()
    svp[n_saved:] = jnp.zeros((svp.shape[0] - n_saved, HS), bf16)
    for copy in own_w:
        copy.wait()
    arrive(WG.at[:, pl.ds(HS, HS)], wrecv.at[0])
    arrive(WD.at[pl.ds(HS, HS), :], wrecv.at[1])
    project(BWD, 0)
    project(BWD, 1)
    b_inv = inverse(ba)
    for at in every:
        bst[:, cols(*at)] = normed(ba, b_inv, at)
    b_aff = jax.nn.sigmoid(mm_nt(bst[...], rt[...]))
    b_gate = jnp.sum(b_one * b_aff, axis=-1, keepdims=True)
    pass_on(FWD, 0)
    have(BWD, 2)
    project(BWD, 2)
    activate(BWD, 0, x)
    activate(BWD, 1, x_dn)
    activate(BWD, 2, x_up)
    for ch in NC[1:]:
        pass_on(FWD, ch)
    project(FWD, 0)
    project(FWD, 1)
    ready(BWD, 2)
    for ch in NC:
        give2(BWD, ch)
    have(BWD, 3)
    project(BWD, 3)
    activate(FWD, 0, x)
    activate(BWD, 3, x_op)
    ready(BWD, 3)
    for ch in NC:
        give3(BWD, ch)
    have(FWD, 2)
    project(FWD, 2)
    activate(FWD, 1, x_dn)
    activate(FWD, 2, x_up)
    ready(BWD, 1)
    for ch in NC:
        give1(BWD, ch)
    have(FWD, 3)
    project(FWD, 3)
    activate(FWD, 3, x_op)
    ready(FWD, 2)
    ready(FWD, 3)
    n = len(NC)
    for ch in NC[: min(3, n)]:
        give3(FWD, ch)
    for ch in NC[: min(2, n)]:
        give2(FWD, ch)
    ready(BWD, 0)
    for ch in NC:
        give0(BWD, ch)
    ready(FWD, 1)
    ready(FWD, 0)
    def push_fwd(ch):
        give1(FWD, ch)
        if ch + 3 < n:
            give3(FWD, ch + 3)
        if ch + 2 < n:
            give2(FWD, ch + 2)

    half = n // 2
    mean = jnp.zeros((TOK, SUB), f32)
    grad_logits = None
    for ch in NC:
        if ch % 2 == 0:
            push_fwd(ch // 2)
        returned(BWD, ch)
        if ch == 0:
            hit = (68 * c + 17 * y).astype(f32) + b_place == iota((TOK, SUB), 1).astype(f32)
            dot = jnp.zeros((TOK, 1), f32)
            for e in range(EXP):
                both = TR[BWD, 0, e, 0:16].astype(f32) + TR[BWD, 1, e, 0:16].astype(f32)
                found = jnp.sum(jnp.where(hit, both[0:1, :], 0.0), axis=-1, keepdims=True)
                dot = dot + b_one[:, e : e + 1] * found
            grad_aff = b_one * (route_scale * dot)
            grad_logits = (grad_aff * b_aff * (1.0 - b_aff)).astype(bf16)
        for at in [(c2, j) for j in range(*OUT[ch]) for c2 in range(2)]:
            grad_n = (route_scale * b_gate) * rows_of(BWD, b_table, at) + mm(grad_logits, rt[:, cols(*at)])
            pre = grad_n * gain[:, cols(*at)].astype(f32)
            gpre[:, cols(*at)] = pre
            mean = mean + pre * ba[:, cols(*at)].astype(f32)
    factor = b_inv * b_inv * (jnp.sum(mean, axis=-1, keepdims=True) * (1.0 / D))
    for ch in NC:
        for c2 in range(2):
            at = wide(c2, OUT[ch])
            grad = b_inv * (gpre[:, at] - ba[:, at].astype(f32) * factor)
            bst[:, at] = (bg[:, at].astype(f32) + grad).astype(bf16)
            bwd_copy(c2, ch).start()
    for ch in range(half, n):
        push_fwd(ch)
        give0(FWD, ch - half)
    for copy in give_w:
        copy.wait_send()
    for m in (BWD, FWD):
        for ch in NC:
            for dy, dc in others:
                send_desc(m, ch, dy, dc).wait_send()
            for copy in ag_own(m, ch) + [ag_on(m, ch), down3(m, ch), up2(m, ch)]:
                copy.wait_send()
        for s in range(4):
            z_copy(m, s).wait_send()
            h_copy(m, s).wait_send()
    for ch in NC:
        for dy, dc in others:
            back_desc(BWD, ch, dy, dc).wait_send()
        down1(BWD, ch).wait_send()

    def finish_fwd(ch):
        returned(FWD, ch)
        for c2 in range(2):
            for j in range(*OUT[ch]):
                at = cols(c2, j)
                fst[:, at] = (
                    fa[:, at].astype(f32) + route_scale * (f_gate * rows_of(FWD, f_table, (c2, j)))
                ).astype(bf16)
            fwd_copy(c2, ch).start()

    for ch in range(n - half, n):
        if n > 2:
            finish_fwd(ch - (n - half))
        give0(FWD, ch)
    for ch in range(half if n > 2 else 0, n):
        finish_fwd(ch)

    for ch in NC:
        for dy, dc in others:
            back_desc(FWD, ch, dy, dc).wait_send()
        down1(FWD, ch).wait_send()
    for ch in NC:
        for c2 in range(2):
            fwd_copy(c2, ch).wait()
            bwd_copy(c2, ch).wait()


def on_device(
    fwd_act, fwd_ids, bwd_act, bwd_ids, bwd_grad, norm_gain, router, w_gate, w_down, saved_gate
):
    D = fwd_act.shape[1]
    HF = D // 2
    n = len(plan(HF)[0])
    saved = saved_gate[0, 0]
    vmem = pl.BlockSpec(memory_space=pltpu.VMEM)
    hbm = pl.BlockSpec(memory_space=pl.ANY)
    dma = pltpu.SemaphoreType.DMA
    V = pltpu.VMEM
    packs = V((2, 2, EXP, PACK, SUB), bf16)
    sums = V((2, BLK, HF), bf16)
    return pl.pallas_call(
        kernel,
        out_shape=[jax.ShapeDtypeStruct((TOK, D), bf16)] * 2,
        in_specs=[hbm, vmem, hbm, vmem, hbm, vmem, vmem] + [hbm] * 3,
        out_specs=[hbm, hbm],
        scratch_shapes=[
            V((TOK, D), bf16),
            V((TOK, D), bf16),
            V((TOK, D), bf16),
            packs,
            packs,
            V((2, 4, BLK, HF), bf16),
            V((HF, 2 * HS), bf16),
            V((2 * HS, HF), bf16),
            V((2, 4, BLK, HS), f32),
            V((2, 4, BLK, HS), f32),
            V((2, 4, BLK, HS), f32),
            V((2, 4, BLK, 2 * HS), bf16),
            sums, sums, sums, sums, sums, sums, sums,
            packs,
            packs,
            V((TOK, D), bf16),
            V((TOK, D), bf16),
            V((TOK, D), f32),
            V((640, HS), bf16),
            V((4, 8, 256), f32),
            dma((4,)), dma((2,)), dma((2,)), dma((2,)),
            dma((2, n)), dma((2, n, 4, 2)), dma((2, n, 2, 4)),
            dma((2, 3, n)), dma((2, 3, n)),
            dma((2, 4)), dma((2, 4)), dma((2, 4)), dma((2, 4)),
            dma((2, 3, n)), dma((2, 3, n)),
            dma((2, n)), dma((2, n, 4, 2)), dma((2, n, 2, 4)),
            dma((2, 2, n)), dma((2, 2, n)),
        ],
        compiler_params=pltpu.CompilerParams(
            collective_id=0, has_side_effects=True, vmem_limit_bytes=56 * 2**20
        ),
    )(
        fwd_act, fwd_ids.reshape(1, TOK), bwd_act, bwd_ids.reshape(1, TOK), bwd_grad, norm_gain,
        router[0].T, w_gate[0], w_down[0], saved,
    )


def solution(mesh):
    return jax.shard_map(
        on_device,
        mesh=mesh,
        in_specs=(
            P(("pp", "ep"), None),
            P(("pp", "ep"), None),
            P(("pp", "ep"), None),
            P(("pp", "ep"), None),
            P(("pp", "ep"), None),
            P("pp", None),
            P("pp", None, None),
            P(("pp", "ep"), None, None),
            P(("pp", "ep"), None, None),
            P("pp", "ep", None, None),
        ),
        out_specs=(P(("pp", "ep"), None), P(("pp", "ep"), None)),
        check_vma=False,
    )
```
